32 devices in a mesh: col: 4 (over y, core), row: 8 (over z, x).
Axes of the slice: x: 2, y: 2, z: 4, core: 2. Of those that a mesh axis runs over, the one named last changes fastest.
Arguments:
- pair_rep: float32 [32, 32, 128], P('row', 'col'), may hold values from -6 to 6
- cotangent: float32 [32, 32, 128], P('row', 'col'), may hold values from -6 to 6
- chain_ids: int32 [32], replicated, may hold values from 0 to 3, never falling along the last dimension, each value on 1 to 16 neighbouring positions
- template: int32 [8, 8], replicated, may hold values from 0 to 1
- norm_gain: float32 [128], replicated, may hold values from 0.25 to 1.75
- w_query: float32 [128, 128], replicated
- w_key: float32 [128, 128], replicated
- w_value: float32 [128, 128], replicated, may hold values from -0.5 to 0.5
- w_gate: float32 [128, 128], replicated, may hold values from -0.5 to 0.5
- gate_bias: float32 [128], replicated, may hold values from -4 to 4
- w_out: float32 [128, 128], replicated, may hold values from -0.5 to 0.5
- w_bias: float32 [4, 128], replicated, may hold values from -0.5 to 0.5
Outputs:
- update: float32 [32, 32, 128], P('row', 'col')
- grad_pair: float32 [32, 32, 128], P('row', 'col')
- grad_query: float32 [128, 128], replicated
- grad_key: float32 [128, 128], replicated
- grad_value: float32 [128, 128], replicated
- grad_gate: float32 [128, 128], replicated
- grad_gate_bias: float32 [128], replicated
- grad_out: float32 [128, 128], replicated
- grad_bias: float32 [4, 128], replicated
- grad_gain: float32 [128], replicated
The draws below stay inside these ranges and needn't reach their ends.
All inputs are finite; a program needn't handle non-finite values.
Results may differ from the reference program's by a relative error of at most 0.0003.
Values sent between devices are 32-bit elements; how exact they have to be, the bound alone decides.
A program may use at most 64 MiB of HBM per device.

```python
import math
import jax
import jax.numpy as jnp
import numpy as np
from jax import lax

C = 128
H = 4
DH = 32
TOKENS = 32
NBLOCKS = 8
MBLOCK = 4
CHAINS = 4


def shared_projection(key):
    raw_values = jax.random.normal(key, (C, C), jnp.float32)
    return jnp.clip(raw_values, -4.0, 4.0) / jnp.sqrt(jnp.float32(C))


def draw_w_key(key, part):
    return shared_projection(key)


def draw_w_query(key, part):
    key = jax.random.fold_in(key, 7)
    own_values = jnp.clip(jax.random.normal(key, (C, C), jnp.float32), -4.0, 4.0) / jnp.sqrt(jnp.float32(C))
    return own_values


def draw_template(key, part):
    key = jax.random.fold_in(key, 5)
    tickets = jax.random.randint(key, (NBLOCKS, NBLOCKS), 0, 3 * NBLOCKS - 3)
    column_index = jnp.arange(NBLOCKS, dtype=jnp.int32)[None, :]
    return (tickets < NBLOCKS - 1 + column_index).astype(jnp.int32)


def block_scale(stream_key, shape, split, least, top_value):
    def one(position, shards_of):
        heights = jax.random.uniform(jax.random.fold_in(jax.random.fold_in(stream_key, 6), position), (shards_of,), jnp.float32, least / len(split), top_value / len(split))
        return jnp.repeat(jnp.exp(heights), shape[position] // shards_of).reshape((-1,) + (1,) * (len(shape) - position - 1))

    gain = one(*split[0])
    for cut in split[1:]:
        gain = gain * one(*cut)
    return gain


def split_up(number_of, total, most, skew):
    portions = [(1 << 20) // math.isqrt(rank ** skew) + 1 for rank in range(2, number_of + 1)]
    spare, given = total - most - (number_of - 1), [1] * (number_of - 1)
    while spare > 0:
        movable = [i for i in range(number_of - 1) if given[i] < most]
        pool, left = sum([portions[i] for i in movable]), spare
        for i in movable:
            more = min(most - given[i], max(1, left * portions[i] // pool), spare)
            given[i] = given[i] + more
            spare = spare - more
    return np.array([most] + given)


def uneven_parts(own_key, number_of, total, most, skew):
    if number_of == 2:
        one = jax.random.randint(own_key, (), max(1, total - most), min(most, total - 1) + 1)
        return jnp.stack([one, total - one])
    tallies = jnp.asarray(split_up(number_of, total, most, skew), jnp.int32)
    pairs = (number_of - 1) // 2
    giver, receiver = tallies[1:1 + 2 * pairs:2], tallies[2:2 + 2 * pairs:2]
    slack = jnp.minimum(giver - 1, most - receiver)
    moved = jax.random.randint(jax.random.fold_in(own_key, 1), (pairs,), 0, 1 << 20) % (slack + 1)
    tallies = tallies.at[1:1 + 2 * pairs:2].set(giver - moved).at[2:2 + 2 * pairs:2].set(receiver + moved)
    return tallies[jax.random.permutation(jax.random.fold_in(own_key, 2), number_of)]


def bell_draw(key, dims, width, reach, cuts=(), kind=jnp.bfloat16):
    array = width * jax.random.normal(key, dims, jnp.float32)
    if cuts:
        array = array * block_scale(key, dims, cuts, -0.22, 0.18)
    return jnp.clip(array, -reach, reach).astype(kind)


def setup_inputs(seed: int = 0) -> dict:
    streams_of = jax.random.split(jax.random.key(seed), 13)
    pair_rep = bell_draw(streams_of[0], (TOKENS, TOKENS, C), 1.0, 6.0, ((0, 8), (1, 4)), jnp.float32)
    cotangent = bell_draw(streams_of[1], (TOKENS, TOKENS, C), 1.0, 6.0, ((0, 8), (1, 4)), jnp.float32)
    chain_ids = jnp.searchsorted(jnp.cumsum(uneven_parts(streams_of[2], CHAINS, TOKENS, TOKENS // 2, 0)), jnp.arange(TOKENS), side="right").astype(jnp.int32)
    template = draw_template(jax.random.fold_in(streams_of[12], 71), 0)
    norm_gain = jnp.clip(1.0 + 0.15 * jax.random.normal(streams_of[4], (C,), jnp.float32), 0.25, 1.75)
    w_query = draw_w_query(jax.random.fold_in(streams_of[12], 71), 0)
    w_key = draw_w_key(jax.random.fold_in(streams_of[12], 71), 0)
    w_value = bell_draw(streams_of[7], (C, C), C ** -0.5, 0.5, (), jnp.float32)
    w_gate = bell_draw(streams_of[8], (C, C), C ** -0.5, 0.5, (), jnp.float32)
    gate_bias = bell_draw(streams_of[9], (C,), 1.0, 4.0, (), jnp.float32)
    w_out = bell_draw(streams_of[10], (C, C), C ** -0.5, 0.5, (), jnp.float32)
    w_bias = bell_draw(streams_of[11], (H, C), C ** -0.5, 0.5, (), jnp.float32)
    return {"pair_rep": pair_rep, "cotangent": cotangent, "chain_ids": chain_ids, "template": template, "norm_gain": norm_gain, "w_query": w_query, "w_key": w_key, "w_value": w_value, "w_gate": w_gate, "gate_bias": gate_bias, "w_out": w_out, "w_bias": w_bias}


HIGHEST = lax.Precision.HIGHEST

def layer_norm(cells, norm_gain):
    center = lax.optimization_barrier(jnp.mean(cells, axis=-1, keepdims=True))
    shifted = cells - center
    spread = lax.optimization_barrier(jnp.mean(shifted * shifted, axis=-1, keepdims=True))
    return shifted * lax.rsqrt(spread + 1e-05) * norm_gain

def column_attention(queries, keys_col, values_col, keep_col, bias_rows):
    scores = jnp.einsum('ihd,khd->ihk', queries, keys_col, precision=HIGHEST) * DH ** (-0.5) + bias_rows
    scores = jnp.where(keep_col[None, None, :] > 0, scores, -1000000000.0)
    highest = lax.stop_gradient(lax.optimization_barrier(jnp.max(scores, axis=2, keepdims=True)))
    weights = jnp.exp(scores - highest)
    normed_weights = weights / lax.optimization_barrier(jnp.sum(weights, axis=2, keepdims=True))
    return jnp.einsum('ihk,khd->ihd', normed_weights, values_col, precision=HIGHEST)

def triangle_update(pair_rep, norm_gain, w_query, w_key, w_value, w_gate, gate_bias, w_out, w_bias, keep_mask):
    normed = layer_norm(pair_rep, norm_gain)

    def project(weight):
        return jnp.einsum('ijc,cd->jid', normed, weight, precision=HIGHEST).reshape(TOKENS, TOKENS, H, DH)
    bias_rows = jnp.einsum('kic,hc->ihk', normed, w_bias, precision=HIGHEST)
    attend = jax.checkpoint(column_attention)
    attended = lax.map(lambda items: attend(items[0], items[1], items[2], items[3], bias_rows), (project(w_query), project(w_key), project(w_value), jnp.transpose(keep_mask)))
    attended = jnp.swapaxes(attended.reshape(TOKENS, TOKENS, C), 0, 1)
    gate = jax.nn.sigmoid(jnp.einsum('ijc,cd->ijd', normed, w_gate, precision=HIGHEST) + gate_bias)
    return jnp.einsum('ijc,cd->ijd', gate * attended, w_out, precision=HIGHEST)

def reference(pair_rep, cotangent, chain_ids, template, norm_gain, w_query, w_key, w_value, w_gate, gate_bias, w_out, w_bias):
    same_chain = (chain_ids[:, None] == chain_ids[None, :]).astype(jnp.int32)
    spread_mask = jnp.repeat(jnp.repeat(template, MBLOCK, axis=0), MBLOCK, axis=1)
    keep_mask = jnp.maximum(same_chain, spread_mask)

    def forward(pair_in, gain_in, query_in, key_in, value_in, gate_in, gate_bias_in, out_in, bias_in):
        return triangle_update(pair_in, gain_in, query_in, key_in, value_in, gate_in, gate_bias_in, out_in, bias_in, keep_mask)
    update, pullback = jax.vjp(forward, pair_rep, norm_gain, w_query, w_key, w_value, w_gate, gate_bias, w_out, w_bias)
    grads = pullback(cotangent)
    return (update, grads[0], grads[2] / TOKENS, grads[3] / TOKENS, grads[4] / TOKENS, grads[5] / TOKENS, grads[6] / TOKENS, grads[7] / TOKENS, grads[8] / TOKENS, grads[1] / TOKENS)
```

```python
import functools

import jax
import jax.numpy as jnp
from jax import lax
from jax.experimental import pallas as pl
from jax.experimental.pallas import tpu as pltpu
from jax.sharding import PartitionSpec as P

HIGHEST = lax.Precision.HIGHEST
NEG_FILL = -1000000000.0


def matmul(left, right):
    return jnp.dot(left, right, precision=HIGHEST, preferred_element_type=jnp.float32)


def attend_dense(queries, keys_col, values_col, bias_rows, keep_col, factor):
    scores = jnp.einsum("ihd,khd->ihk", queries, keys_col, precision=HIGHEST) * factor + bias_rows
    scores = jnp.where(keep_col[None, None, :], scores, NEG_FILL)
    highest = jnp.max(scores, axis=2, keepdims=True)
    weights = jnp.exp(scores - highest)
    normed_weights = weights / jnp.sum(weights, axis=2, keepdims=True)
    output = jnp.einsum("ihk,khd->ihd", normed_weights, values_col, precision=HIGHEST)
    return (output, normed_weights)


def attend_dense_back(queries, keys_col, values_col, normed_weights, output, d_output, factor):
    d_weights = jnp.einsum("ihd,khd->ihk", d_output, values_col, precision=HIGHEST)
    centred = jnp.sum(d_output * output, axis=2, keepdims=True)
    d_scores = normed_weights * (d_weights - centred)
    d_query = jnp.einsum("ihk,khd->ihd", d_scores, keys_col, precision=HIGHEST) * factor
    d_key = jnp.einsum("ihk,ihd->khd", d_scores, queries, precision=HIGHEST) * factor
    d_value = jnp.einsum("ihk,ihd->khd", normed_weights, d_output, precision=HIGHEST)
    return (d_query, d_key, d_value, d_scores)


def body_collective(
    pair_rep,
    cotangent,
    chain_ids,
    template,
    norm_gain,
    w_query,
    w_key,
    w_value,
    w_gate,
    gate_bias,
    w_out,
    w_bias,
):
    column_cells, upstream = (
        lax.all_to_all(pair_rep, "row", split_axis=1, concat_axis=0, tiled=True),
        lax.all_to_all(cotangent, "row", split_axis=1, concat_axis=0, tiled=True),
    )
    tokens, cols, width = column_cells.shape
    head_count = w_bias.shape[0]
    head_depth = width // head_count
    factor = head_depth ** (-0.5)
    row_count = lax.axis_size("row")
    linear = lax.axis_index("col") * row_count + lax.axis_index("row")
    first_col = linear * cols
    own_chain = lax.dynamic_slice_in_dim(chain_ids, first_col, cols, 0)
    same_chain = chain_ids[:, None] == own_chain[None, :]
    block_count = template.shape[0]
    block_width = tokens // block_count
    own_block = (first_col + jnp.arange(cols, dtype=jnp.int32)) // block_width
    picker = (jnp.arange(block_count, dtype=jnp.int32)[:, None] == own_block[None, :]).astype(
        jnp.int32
    )
    block_keep = jnp.sum(template[:, :, None] * picker[None, :, :], axis=1)
    keep_mask = same_chain | (jnp.repeat(block_keep, block_width, axis=0) > 0)
    cells = column_cells.reshape(tokens * cols, width)
    center = jnp.mean(cells, axis=-1, keepdims=True)
    shifted = cells - center
    spread = jnp.mean(shifted * shifted, axis=-1, keepdims=True)
    inverse = lax.rsqrt(spread + 1e-05)
    scaled = shifted * inverse
    normed = scaled * norm_gain
    queries = matmul(normed, w_query).reshape(tokens, cols, head_count, head_depth)
    keys_all = matmul(normed, w_key).reshape(tokens, cols, head_count, head_depth)
    values_all = matmul(normed, w_value).reshape(tokens, cols, head_count, head_depth)
    gate = jax.nn.sigmoid(matmul(normed, w_gate) + gate_bias)
    normed_cols = normed.reshape(tokens, cols, width)
    bias_piece = jnp.einsum("ktc,hc->thk", normed_cols, w_bias, precision=HIGHEST)
    bias_rows = lax.all_gather(bias_piece, ("col", "row"), axis=0, tiled=True)
    actives = []
    slot = 0
    keep_col = keep_mask[:, slot]
    active = jnp.any(keep_col.reshape(block_count, block_width), axis=1)
    actives.append(active)
    attended_slot, kept_stat = attend_dense(
        queries[:, slot], keys_all[:, slot], values_all[:, slot], bias_rows, keep_col, factor
    )
    outputs = [attended_slot]
    saved = [kept_stat]
    attended = jnp.stack(outputs, axis=1).reshape(tokens * cols, width)
    gated = gate * attended
    update_cols = matmul(gated, w_out).reshape(tokens, cols, width)
    update_block = lax.all_to_all(update_cols, "row", split_axis=0, concat_axis=1, tiled=True)
    d_cells = upstream.reshape(tokens * cols, width)
    d_gated = matmul(d_cells, jnp.transpose(w_out))
    grad_out_w = matmul(jnp.transpose(gated), d_cells)
    d_attended = (d_gated * gate).reshape(tokens, cols, head_count, head_depth)
    d_gate_pre = d_gated * attended * gate * (1.0 - gate)
    slot = 0
    query_grad, key_grad, value_grad, score_grad = attend_dense_back(
        queries[:, slot],
        keys_all[:, slot],
        values_all[:, slot],
        saved[slot],
        outputs[slot],
        d_attended[:, slot],
        factor,
    )
    d_queries = [query_grad]
    d_keys = [key_grad]
    d_values = [value_grad]
    d_query = jnp.stack(d_queries, axis=1).reshape(tokens * cols, width)
    d_key = jnp.stack(d_keys, axis=1).reshape(tokens * cols, width)
    d_value = jnp.stack(d_values, axis=1).reshape(tokens * cols, width)
    bias_grad = lax.psum_scatter(score_grad, ("col", "row"), scatter_dimension=0, tiled=True)
    bias_back = jnp.einsum("thk,hc->ktc", bias_grad, w_bias, precision=HIGHEST).reshape(
        tokens * cols, width
    )
    grad_bias_w = jnp.einsum("thk,ktc->hc", bias_grad, normed_cols, precision=HIGHEST)
    d_normed = (
        matmul(d_query, jnp.transpose(w_query))
        + matmul(d_key, jnp.transpose(w_key))
        + matmul(d_value, jnp.transpose(w_value))
        + matmul(d_gate_pre, jnp.transpose(w_gate))
        + bias_back
    )
    grad_query_w = matmul(jnp.transpose(normed), d_query)
    grad_key_w = matmul(jnp.transpose(normed), d_key)
    grad_value_w = matmul(jnp.transpose(normed), d_value)
    grad_gate_w = matmul(jnp.transpose(normed), d_gate_pre)
    grad_gate_shift = jnp.sum(d_gate_pre, axis=0)
    grad_gain_w = jnp.sum(d_normed * scaled, axis=0)
    d_scaled = d_normed * norm_gain
    mean_term = jnp.mean(d_scaled, axis=-1, keepdims=True)
    cross_term = jnp.mean(d_scaled * scaled, axis=-1, keepdims=True)
    d_input = inverse * (d_scaled - mean_term - scaled * cross_term)
    grad_block = lax.all_to_all(
        d_input.reshape(tokens, cols, width), "row", split_axis=0, concat_axis=1, tiled=True
    )
    summed = lax.psum(
        (
            grad_query_w,
            grad_key_w,
            grad_value_w,
            grad_gate_w,
            grad_gate_shift,
            grad_out_w,
            grad_bias_w,
            grad_gain_w,
        ),
        ("col", "row"),
    )
    return (
        update_block,
        grad_block,
        summed[0] / tokens,
        summed[1] / tokens,
        summed[2] / tokens,
        summed[3] / tokens,
        summed[4] / tokens,
        summed[5] / tokens,
        summed[6] / tokens,
        summed[7] / tokens,
    )


MESH = pl.DeviceIdType.MESH
LANES = 128
SUBLANES = 8
MATRICES = 5
CORE_SETS = ((0, 3), (3, 2))
CELLS, BIAS, UPDATE, CELL_GRAD, SCORE_GRAD, SMALL, SCATTER, GATHER, FORWARD, PAIR = range(10)


def dot(left, right, left_dim=1, right_dim=0):
    return lax.dot_general(
        left,
        right,
        (((left_dim,), (right_dim,)), ((), ())),
        precision=HIGHEST,
        preferred_element_type=jnp.float32,
    )


def layer_norm_parts(cells):
    shifted = cells - jnp.mean(cells, axis=-1, keepdims=True)
    inverse = lax.rsqrt(jnp.mean(shifted * shifted, axis=-1, keepdims=True) + 1e-05)
    return shifted * inverse, inverse


def layer_norm_back(d_scaled, scaled, inverse):
    mean_term = jnp.mean(d_scaled, axis=-1, keepdims=True)
    cross_term = jnp.mean(d_scaled * scaled, axis=-1, keepdims=True)
    return inverse * (d_scaled - mean_term - scaled * cross_term)


def fused_kernel(
    row_count, col_count, tokens, heads, blocks,
    pair_ref, cot_ref, chain_ref, template_ref, gain_ref,
    wq_ref, wk_ref, wv_ref, wg_ref, gate_bias_ref, wo_ref, wb_ref,
    update_out, pair_out, query_out, key_out, value_out, gate_out, gate_bias_out, wo_out, bias_out, gain_out,
    cell_send, cell_recv, bias_send, bias_recv, bias_full, update_send, update_recv,
    grad_send, grad_recv, score_send, score_recv, small_send, small_recv,
    parts, pair_recv, scatter_recv, gather_send, final, send_sem, recv_sem,
):
    width = LANES
    depth = width // heads
    factor = depth ** (-0.5)
    rows = tokens // row_count
    cols = tokens // col_count
    count = row_count * col_count
    half_cols = col_count // 2
    chips = count // 2
    tile = width // chips
    row = lax.axis_index("row")
    col = lax.axis_index("col")
    me = row * col_count + col
    core = lax.rem(col, 2)
    chip = row * half_cols + col // 2
    partner = (col + 1 - 2 * core, row)

    def device(index):
        return (lax.rem(index, col_count), index // col_count)

    def remote(src, dst, kind, target):
        return pltpu.make_async_remote_copy(
            src_ref=src, dst_ref=dst, send_sem=send_sem.at[kind], recv_sem=recv_sem.at[kind],
            device_id=target, device_id_type=MESH,
        )

    def to_all(make):
        def step(distance, carry):
            make(lax.rem(me + distance, count)).start()
            return carry
        lax.fori_loop(1, count, step, 0)

    def to_rows(make):
        def step(distance, carry):
            make(lax.rem(row + distance, row_count)).start()
            return carry
        lax.fori_loop(1, row_count, step, 0)

    def wait_for(ref, sem, kind):
        pltpu.make_async_copy(ref, ref, sem.at[kind]).wait()

    barrier = pltpu.get_barrier_semaphore()

    def greet(distance, carry):
        pl.semaphore_signal(
            barrier, inc=1, device_id=device(lax.rem(me + distance, count)), device_id_type=MESH
        )
        return carry

    lax.fori_loop(1, count, greet, 0)

    for slot in range(cols):
        cell_send[slot, :rows, :] = pair_ref[:, slot, :]
        cell_send[slot, rows:, :] = cot_ref[:, slot, :]
    gain = gain_ref[...]
    block_scaled, block_inverse = layer_norm_parts(pair_ref[...].reshape(rows * cols, width))
    spread_bias = jnp.broadcast_to(wb_ref[...][:, None, :], (heads, tokens, width)).reshape(
        heads * tokens, width
    )
    products = dot(block_scaled * gain, spread_bias, 1, 1).reshape(rows, cols, heads * tokens)
    lane_token = lax.broadcasted_iota(jnp.int32, (1, cols, heads * tokens), 2) & (tokens - 1)
    block_col = lax.broadcasted_iota(jnp.int32, (1, cols, heads * tokens), 1) + col * cols
    own_lane = lane_token == block_col
    bias_send[...] = jnp.sum(jnp.where(own_lane, products, 0.0), axis=1)
    pl.semaphore_wait(barrier, count - 1)

    to_rows(lambda r: remote(cell_send.at[r], cell_recv.at[row], CELLS, (col, r)))
    to_all(lambda d: remote(bias_send, bias_recv.at[me], BIAS, device(d)))
    cell_recv[row] = cell_send[row]
    bias_recv[me] = bias_send[...]

    own = col * cols + row
    token_shift = (tokens // blocks).bit_length() - 1
    chain_row = chain_ref[...].astype(jnp.float32)
    square_row = lax.broadcasted_iota(jnp.int32, (tokens, tokens), 0)
    square_col = lax.broadcasted_iota(jnp.int32, (tokens, tokens), 1)
    chain_all = jnp.broadcast_to(chain_row, (tokens, tokens))
    chain_col = jnp.sum(jnp.where(square_row == square_col, chain_all, 0.0), axis=1, keepdims=True)
    own_chain = jnp.sum(jnp.where(square_col == own, chain_all, 0.0), axis=1, keepdims=True)
    spread_row = (
        lax.broadcasted_iota(jnp.int32, (tokens, blocks), 0) >> token_shift
        == lax.broadcasted_iota(jnp.int32, (tokens, blocks), 1)
    ).astype(jnp.float32)
    spread_template = dot(spread_row, template_ref[...].astype(jnp.float32))
    block_lane = lax.broadcasted_iota(jnp.int32, (tokens, blocks), 1)
    template_col = jnp.sum(
        jnp.where(block_lane == own >> token_shift, spread_template, 0.0), axis=1, keepdims=True
    )
    keep = (chain_col == own_chain) | (template_col > 0.5)
    depth_shift = depth.bit_length() - 1
    head_mask = (
        lax.broadcasted_iota(jnp.int32, (heads, 1, width), 2) >> depth_shift
        == lax.broadcasted_iota(jnp.int32, (heads, 1, width), 0)
    ).astype(jnp.float32)

    def by_head(array):
        return (array[None] * head_mask).reshape(heads * tokens, width)

    def own_head(array):
        return jnp.sum(array.reshape(heads, tokens, width) * head_mask, axis=0)

    wait_for(cell_recv.at[pl.ds(0, row_count - 1)], recv_sem, CELLS)
    cells = jnp.concatenate([cell_recv[r, :rows, :] for r in range(row_count)], axis=0)
    upstream = jnp.concatenate([cell_recv[r, rows:, :] for r in range(row_count)], axis=0)
    scaled, inverse = layer_norm_parts(cells)
    normed = scaled * gain
    queries = dot(normed, wq_ref[...])
    keys = dot(normed, wk_ref[...])
    values = dot(normed, wv_ref[...])
    gate = jax.nn.sigmoid(dot(normed, wg_ref[...]) + gate_bias_ref[...])
    d_gated = dot(upstream, wo_ref[...], 1, 1)
    d_attended_heads = by_head(d_gated * gate)
    query_heads = by_head(queries)
    scores = dot(keys, query_heads, 1, 1) * factor
    d_weights = dot(values, d_attended_heads, 1, 1)

    wait_for(bias_recv.at[pl.ds(0, count - 1)], recv_sem, BIAS)
    bias_rows = jnp.sum(bias_recv[...].reshape(row_count, col_count, rows, heads * tokens), axis=1)
    for r in range(row_count):
        bias_full[r * rows : (r + 1) * rows, :] = bias_rows[r]
    scores = jnp.where(keep, scores + bias_full[...], NEG_FILL)
    weights = jnp.exp(scores - jnp.max(scores, axis=0, keepdims=True))
    weights = weights / jnp.sum(weights, axis=0, keepdims=True)
    d_scores = weights * (d_weights - jnp.sum(weights * d_weights, axis=0, keepdims=True))
    for r in range(row_count):
        score_send[r] = d_scores[r * rows : (r + 1) * rows, :]
    to_all(lambda d: remote(score_send.at[d // col_count], score_recv.at[me], SCORE_GRAD, device(d)))
    score_recv[me] = score_send[row]

    def share(index, grad):
        parts[index] = grad
        owner = 0 if index < CORE_SETS[0][1] else 1

        @pl.when(core != owner)
        def _():
            remote(parts.at[index], pair_recv.at[index], PAIR + index, partner).start()

    attended = own_head(dot(weights, values, 0, 0))
    gated = gate * attended
    d_gate = d_gated * attended * gate * (1.0 - gate)
    d_query = own_head(dot(d_scores, keys, 0, 0)) * factor
    d_key = dot(d_scores, query_heads) * factor
    d_value = dot(weights, d_attended_heads)
    share(3, dot(normed, d_query, 0, 0))
    share(4, dot(normed, d_key, 0, 0))
    share(0, dot(gated, upstream, 0, 0))
    share(1, dot(normed, d_gate, 0, 0))
    share(2, dot(normed, d_value, 0, 0))

    for which in range(2):
        first, number = CORE_SETS[which]

        @pl.when(core == which)
        def _(first=first, number=number):
            for index in range(first, first + number):
                wait_for(pair_recv.at[index], recv_sem, PAIR + index)
                parts[index] = parts[index] + pair_recv[index]

            def step(distance, carry):
                target = lax.rem(chip + distance, chips)
                remote(
                    parts.at[pl.ds(first, number), pl.ds(pl.multiple_of(target * tile, tile), tile), :],
                    scatter_recv.at[chip, pl.ds(0, number)],
                    SCATTER,
                    (lax.rem(target, half_cols) * 2 + core, target // half_cols),
                ).start()
                return carry

            lax.fori_loop(1, chips, step, 0)

    d_normed = (
        dot(d_query, wq_ref[...], 1, 1)
        + dot(d_key, wk_ref[...], 1, 1)
        + dot(d_value, wv_ref[...], 1, 1)
        + dot(d_gate, wg_ref[...], 1, 1)
    )
    d_cells = layer_norm_back(d_normed * gain, scaled, inverse)
    for r in range(row_count):
        grad_send[r] = d_cells[r * rows : (r + 1) * rows, :]
    to_rows(lambda r: remote(grad_send.at[r], grad_recv.at[row], CELL_GRAD, (col, r)))
    grad_recv[row] = grad_send[row]
    update = dot(gated, wo_ref[...])
    for r in range(row_count):
        update_send[r] = update[r * rows : (r + 1) * rows, :]
    to_rows(lambda r: remote(update_send.at[r], update_recv.at[row], UPDATE, (col, r)))
    update_recv[row] = update_send[row]

    wait_for(score_recv.at[pl.ds(0, count - 1)], recv_sem, SCORE_GRAD)
    bias_grad = jnp.sum(score_recv[...], axis=0)
    picked = jnp.where(own_lane, bias_grad[:, None, :], 0.0).reshape(rows * cols, heads * tokens)
    bias_sums = dot(picked, block_scaled, 0, 0).reshape(heads, tokens, width)
    small_send[0:heads, :] = jnp.sum(bias_sums, axis=1)
    small_send[heads : heads + 1, :] = jnp.sum(d_gate, axis=0, keepdims=True)
    small_send[heads + 1 : heads + 2, :] = jnp.sum(d_normed * scaled, axis=0, keepdims=True)
    to_all(lambda d: remote(small_send, small_recv.at[me], SMALL, device(d)))
    small_recv[me] = small_send[...]
    bias_part = layer_norm_back(dot(picked, spread_bias) * gain, block_scaled, block_inverse).reshape(
        rows, cols, width
    )

    share_scale = 1.0 / tokens
    for which in range(2):
        first, number = CORE_SETS[which]

        @pl.when(core == which)
        def _(first=first, number=number):
            mine = pl.ds(pl.multiple_of(chip * tile, tile), tile)
            wait_for(scatter_recv.at[pl.ds(0, chips - 1), pl.ds(0, number)], recv_sem, SCATTER)
            scatter_recv[chip, pl.ds(0, number)] = parts[pl.ds(first, number), mine, :]
            total = jnp.sum(scatter_recv[:, pl.ds(0, number)], axis=0) * share_scale
            gather_send[pl.ds(0, number)] = total
            final[pl.ds(first, number), mine, :] = total

            def step(distance, carry):
                target = lax.rem(chip + distance, chips)
                remote(
                    gather_send.at[pl.ds(0, number)],
                    final.at[pl.ds(first, number), mine, :],
                    GATHER,
                    (lax.rem(target, half_cols) * 2 + core, target // half_cols),
                ).start()
                return carry

            lax.fori_loop(1, chips, step, 0)

    wait_for(grad_recv.at[pl.ds(0, row_count - 1)], recv_sem, CELL_GRAD)
    wait_for(update_recv.at[pl.ds(0, row_count - 1)], recv_sem, UPDATE)
    for slot in range(cols):
        pair_out[:, slot, :] = grad_recv[slot] + bias_part[:, slot, :]
        update_out[:, slot, :] = update_recv[slot]
    wait_for(small_recv.at[pl.ds(0, count - 1)], recv_sem, SMALL)
    small = jnp.sum(small_recv[...], axis=0) * share_scale
    bias_out[...] = small[:heads] * gain
    gate_bias_out[...] = small[heads : heads + 1]
    gain_out[...] = small[heads + 1 : heads + 2] + jnp.sum(
        small[:heads] * wb_ref[...], axis=0, keepdims=True
    )

    for which in range(2):
        first, number = CORE_SETS[which]
        other_first, other_number = CORE_SETS[1 - which]

        @pl.when(core == which)
        def _(first=first, number=number, other_first=other_first, other_number=other_number):
            some = scatter_recv.at[pl.ds(0, chips - 1), pl.ds(0, number)]
            wait_for(some, recv_sem, GATHER)
            forward = final.at[pl.ds(first, number)]
            remote(forward, forward, FORWARD, partner).start()
            wait_for(final.at[pl.ds(other_first, other_number)], recv_sem, FORWARD)
            wait_for(some, send_sem, SCATTER)
            wait_for(some, send_sem, GATHER)
            wait_for(forward, send_sem, FORWARD)
            for index in range(other_first, other_first + other_number):
                wait_for(parts.at[index], send_sem, PAIR + index)

    wo_out[...] = final[0]
    gate_out[...] = final[1]
    value_out[...] = final[2]
    query_out[...] = final[3]
    key_out[...] = final[4]
    wait_for(cell_recv.at[pl.ds(0, row_count - 1)], send_sem, CELLS)
    wait_for(bias_recv.at[pl.ds(0, count - 1)], send_sem, BIAS)
    wait_for(update_recv.at[pl.ds(0, row_count - 1)], send_sem, UPDATE)
    wait_for(grad_recv.at[pl.ds(0, row_count - 1)], send_sem, CELL_GRAD)
    wait_for(score_recv.at[pl.ds(0, count - 1)], send_sem, SCORE_GRAD)
    wait_for(small_recv.at[pl.ds(0, count - 1)], send_sem, SMALL)


def body_fused(
    row_count, col_count, tokens,
    pair_rep, cotangent, chain_ids, template, norm_gain,
    w_query, w_key, w_value, w_gate, gate_bias, w_out, w_bias,
):
    rows, cols, width = pair_rep.shape
    heads = w_bias.shape[0]
    count = row_count * col_count
    chips = count // 2
    tile = width // chips
    number = CORE_SETS[0][1]
    f32 = jnp.float32

    def shape(*dims):
        return jax.ShapeDtypeStruct(dims, f32)

    def vmem(*dims):
        return pltpu.VMEM(dims, f32)

    square = shape(width, width)
    out = pl.pallas_call(
        functools.partial(fused_kernel, row_count, col_count, tokens, heads, template.shape[0]),
        out_shape=(
            shape(rows, cols, width), shape(rows, cols, width), square, square, square, square,
            shape(1, width), square, shape(heads, width), shape(1, width),
        ),
        in_specs=[pl.BlockSpec(memory_space=pltpu.VMEM)] * 12,
        out_specs=[pl.BlockSpec(memory_space=pltpu.VMEM)] * 10,
        scratch_shapes=[
            vmem(cols, 2 * rows, width), vmem(row_count, 2 * rows, width),
            vmem(rows, width), vmem(count, rows, width), vmem(tokens, width),
            vmem(row_count, rows, width), vmem(row_count, rows, width),
            vmem(row_count, rows, width), vmem(row_count, rows, width),
            vmem(row_count, rows, width), vmem(count, rows, width),
            vmem(heads + 2, width), vmem(count, heads + 2, width),
            vmem(MATRICES, width, width), vmem(MATRICES, width, width),
            vmem(chips, number, tile, width), vmem(number, tile, width), vmem(MATRICES, width, width),
            pltpu.SemaphoreType.DMA((PAIR + MATRICES,)),
            pltpu.SemaphoreType.DMA((PAIR + MATRICES,)),
        ],
        compiler_params=pltpu.CompilerParams(
            collective_id=0, has_side_effects=True, vmem_limit_bytes=32 * 1024 * 1024
        ),
        name="triangle",
    )(
        pair_rep, cotangent, chain_ids.reshape(1, -1), template, norm_gain.reshape(1, -1),
        w_query, w_key, w_value, w_gate, gate_bias.reshape(1, -1), w_out, w_bias,
    )
    return out[:6] + (out[6].reshape(width),) + out[7:9] + (out[9].reshape(width),)


def body(*arrays):
    row_count, col_count = lax.axis_size("row"), lax.axis_size("col")
    rows, cols, width = arrays[0].shape
    tokens = rows * row_count
    heads = arrays[11].shape[0]
    chips = row_count * col_count // 2
    fits = heads * tokens == LANES and width == LANES and width % (chips * SUBLANES) == 0
    if fits and cols == row_count and col_count % 2 == 0:
        return body_fused(row_count, col_count, tokens, *arrays)
    return body_collective(*arrays)


def solution(mesh):
    in_specs = (
        P("row", "col", None),
        P("row", "col", None),
        P(),
        P(),
        P(),
        P(),
        P(),
        P(),
        P(),
        P(),
        P(),
        P(),
    )
    out_specs = (
        P("row", "col", None),
        P("row", "col", None),
        P(),
        P(),
        P(),
        P(),
        P(),
        P(),
        P(),
        P(),
    )
    return jax.shard_map(body, mesh=mesh, in_specs=in_specs, out_specs=out_specs, check_vma=False)
```

```python
import functools

import jax
import jax.numpy as jnp
from jax import lax
from jax.experimental import pallas as pl
from jax.experimental.pallas import tpu as pltpu
from jax.sharding import PartitionSpec as P

HIGHEST = lax.Precision.HIGHEST
NEG_FILL = -1000000000.0


def matmul(left, right):
    return jnp.dot(left, right, precision=HIGHEST, preferred_element_type=jnp.float32)


def attend_dense(queries, keys_col, values_col, bias_rows, keep_col, factor):
    scores = jnp.einsum("ihd,khd->ihk", queries, keys_col, precision=HIGHEST) * factor + bias_rows
    scores = jnp.where(keep_col[None, None, :], scores, NEG_FILL)
    highest = jnp.max(scores, axis=2, keepdims=True)
    weights = jnp.exp(scores - highest)
    normed_weights = weights / jnp.sum(weights, axis=2, keepdims=True)
    output = jnp.einsum("ihk,khd->ihd", normed_weights, values_col, precision=HIGHEST)
    return (output, normed_weights)


def attend_dense_back(queries, keys_col, values_col, normed_weights, output, d_output, factor):
    d_weights = jnp.einsum("ihd,khd->ihk", d_output, values_col, precision=HIGHEST)
    centred = jnp.sum(d_output * output, axis=2, keepdims=True)
    d_scores = normed_weights * (d_weights - centred)
    d_query = jnp.einsum("ihk,khd->ihd", d_scores, keys_col, precision=HIGHEST) * factor
    d_key = jnp.einsum("ihk,ihd->khd", d_scores, queries, precision=HIGHEST) * factor
    d_value = jnp.einsum("ihk,ihd->khd", normed_weights, d_output, precision=HIGHEST)
    return (d_query, d_key, d_value, d_scores)


def body_collective(
    pair_rep,
    cotangent,
    chain_ids,
    template,
    norm_gain,
    w_query,
    w_key,
    w_value,
    w_gate,
    gate_bias,
    w_out,
    w_bias,
):
    column_cells, upstream = (
        lax.all_to_all(pair_rep, "row", split_axis=1, concat_axis=0, tiled=True),
        lax.all_to_all(cotangent, "row", split_axis=1, concat_axis=0, tiled=True),
    )
    tokens, cols, width = column_cells.shape
    head_count = w_bias.shape[0]
    head_depth = width // head_count
    factor = head_depth ** (-0.5)
    row_count = lax.axis_size("row")
    linear = lax.axis_index("col") * row_count + lax.axis_index("row")
    first_col = linear * cols
    own_chain = lax.dynamic_slice_in_dim(chain_ids, first_col, cols, 0)
    same_chain = chain_ids[:, None] == own_chain[None, :]
    block_count = template.shape[0]
    block_width = tokens // block_count
    own_block = (first_col + jnp.arange(cols, dtype=jnp.int32)) // block_width
    picker = (jnp.arange(block_count, dtype=jnp.int32)[:, None] == own_block[None, :]).astype(
        jnp.int32
    )
    block_keep = jnp.sum(template[:, :, None] * picker[None, :, :], axis=1)
    keep_mask = same_chain | (jnp.repeat(block_keep, block_width, axis=0) > 0)
    cells = column_cells.reshape(tokens * cols, width)
    center = jnp.mean(cells, axis=-1, keepdims=True)
    shifted = cells - center
    spread = jnp.mean(shifted * shifted, axis=-1, keepdims=True)
    inverse = lax.rsqrt(spread + 1e-05)
    scaled = shifted * inverse
    normed = scaled * norm_gain
    queries = matmul(normed, w_query).reshape(tokens, cols, head_count, head_depth)
    keys_all = matmul(normed, w_key).reshape(tokens, cols, head_count, head_depth)
    values_all = matmul(normed, w_value).reshape(tokens, cols, head_count, head_depth)
    gate = jax.nn.sigmoid(matmul(normed, w_gate) + gate_bias)
    normed_cols = normed.reshape(tokens, cols, width)
    bias_piece = jnp.einsum("ktc,hc->thk", normed_cols, w_bias, precision=HIGHEST)
    bias_rows = lax.all_gather(bias_piece, ("col", "row"), axis=0, tiled=True)
    actives = []
    slot = 0
    keep_col = keep_mask[:, slot]
    active = jnp.any(keep_col.reshape(block_count, block_width), axis=1)
    actives.append(active)
    attended_slot, kept_stat = attend_dense(
        queries[:, slot], keys_all[:, slot], values_all[:, slot], bias_rows, keep_col, factor
    )
    outputs = [attended_slot]
    saved = [kept_stat]
    attended = jnp.stack(outputs, axis=1).reshape(tokens * cols, width)
    gated = gate * attended
    update_cols = matmul(gated, w_out).reshape(tokens, cols, width)
    update_block = lax.all_to_all(update_cols, "row", split_axis=0, concat_axis=1, tiled=True)
    d_cells = upstream.reshape(tokens * cols, width)
    d_gated = matmul(d_cells, jnp.transpose(w_out))
    grad_out_w = matmul(jnp.transpose(gated), d_cells)
    d_attended = (d_gated * gate).reshape(tokens, cols, head_count, head_depth)
    d_gate_pre = d_gated * attended * gate * (1.0 - gate)
    slot = 0
    query_grad, key_grad, value_grad, score_grad = attend_dense_back(
        queries[:, slot],
        keys_all[:, slot],
        values_all[:, slot],
        saved[slot],
        outputs[slot],
        d_attended[:, slot],
        factor,
    )
    d_queries = [query_grad]
    d_keys = [key_grad]
    d_values = [value_grad]
    d_query = jnp.stack(d_queries, axis=1).reshape(tokens * cols, width)
    d_key = jnp.stack(d_keys, axis=1).reshape(tokens * cols, width)
    d_value = jnp.stack(d_values, axis=1).reshape(tokens * cols, width)
    bias_grad = lax.psum_scatter(score_grad, ("col", "row"), scatter_dimension=0, tiled=True)
    bias_back = jnp.einsum("thk,hc->ktc", bias_grad, w_bias, precision=HIGHEST).reshape(
        tokens * cols, width
    )
    grad_bias_w = jnp.einsum("thk,ktc->hc", bias_grad, normed_cols, precision=HIGHEST)
    d_normed = (
        matmul(d_query, jnp.transpose(w_query))
        + matmul(d_key, jnp.transpose(w_key))
        + matmul(d_value, jnp.transpose(w_value))
        + matmul(d_gate_pre, jnp.transpose(w_gate))
        + bias_back
    )
    grad_query_w = matmul(jnp.transpose(normed), d_query)
    grad_key_w = matmul(jnp.transpose(normed), d_key)
    grad_value_w = matmul(jnp.transpose(normed), d_value)
    grad_gate_w = matmul(jnp.transpose(normed), d_gate_pre)
    grad_gate_shift = jnp.sum(d_gate_pre, axis=0)
    grad_gain_w = jnp.sum(d_normed * scaled, axis=0)
    d_scaled = d_normed * norm_gain
    mean_term = jnp.mean(d_scaled, axis=-1, keepdims=True)
    cross_term = jnp.mean(d_scaled * scaled, axis=-1, keepdims=True)
    d_input = inverse * (d_scaled - mean_term - scaled * cross_term)
    grad_block = lax.all_to_all(
        d_input.reshape(tokens, cols, width), "row", split_axis=0, concat_axis=1, tiled=True
    )
    summed = lax.psum(
        (
            grad_query_w,
            grad_key_w,
            grad_value_w,
            grad_gate_w,
            grad_gate_shift,
            grad_out_w,
            grad_bias_w,
            grad_gain_w,
        ),
        ("col", "row"),
    )
    return (
        update_block,
        grad_block,
        summed[0] / tokens,
        summed[1] / tokens,
        summed[2] / tokens,
        summed[3] / tokens,
        summed[4] / tokens,
        summed[5] / tokens,
        summed[6] / tokens,
        summed[7] / tokens,
    )


MESH = pl.DeviceIdType.MESH
LANES = 128
SUBLANES = 8
MATRICES = 5
CORE_SETS = ((0, 3), (3, 2))
CELLS, BIAS, UPDATE, CELL_GRAD, SCORE_GRAD, SMALL, SCATTER, GATHER, FORWARD, PAIR = range(10)


def dot(left, right, left_dim=1, right_dim=0):
    return lax.dot_general(
        left,
        right,
        (((left_dim,), (right_dim,)), ((), ())),
        precision=HIGHEST,
        preferred_element_type=jnp.float32,
    )


def layer_norm_parts(cells):
    shifted = cells - jnp.mean(cells, axis=-1, keepdims=True)
    inverse = lax.rsqrt(jnp.mean(shifted * shifted, axis=-1, keepdims=True) + 1e-05)
    return shifted * inverse, inverse


def layer_norm_back(d_scaled, scaled, inverse):
    mean_term = jnp.mean(d_scaled, axis=-1, keepdims=True)
    cross_term = jnp.mean(d_scaled * scaled, axis=-1, keepdims=True)
    return inverse * (d_scaled - mean_term - scaled * cross_term)


def fused_kernel(
    row_count, col_count, tokens, heads, blocks,
    pair_in, cot_in, chain_in, template_in, gain_in,
    wq_in, wk_in, wv_in, wg_in, gate_bias_in, wo_in, wb_in,
    update_hbm, pair_hbm, query_hbm, key_hbm, value_hbm, gate_hbm, gate_bias_hbm, wo_hbm, bias_hbm, gain_hbm,
    cell_send, cell_recv, bias_send, bias_recv, bias_full, update_send, update_recv,
    grad_send, grad_recv, score_send, score_recv, small_send, small_recv,
    parts, pair_recv, scatter_recv, gather_send, final,
    pair_ref, cot_ref, chain_ref, template_ref, gain_ref,
    wq_ref, wk_ref, wv_ref, wg_ref, gate_bias_ref, wo_ref, wb_ref,
    update_out, pair_out, bias_out, gate_bias_out, gain_out,
    send_sem, recv_sem, load_sem, store_sem,
):
    loads = [
        pltpu.make_async_copy(source, held, load_sem.at[index])
        for index, (source, held) in enumerate(
            (
                (pair_in, pair_ref), (cot_in, cot_ref), (gain_in, gain_ref), (wb_in, wb_ref),
                (chain_in, chain_ref), (template_in, template_ref), (wq_in, wq_ref), (wk_in, wk_ref),
                (wv_in, wv_ref), (wg_in, wg_ref), (gate_bias_in, gate_bias_ref), (wo_in, wo_ref),
            )
        )
    ]
    for load in loads:
        load.start()
    stores = []

    def store(held, target):
        copy = pltpu.make_async_copy(held, target, store_sem.at[len(stores)])
        copy.start()
        stores.append(copy)
    width = LANES
    depth = width // heads
    factor = depth ** (-0.5)
    rows = tokens // row_count
    cols = tokens // col_count
    count = row_count * col_count
    half_cols = col_count // 2
    chips = count // 2
    tile = width // chips
    row = lax.axis_index("row")
    col = lax.axis_index("col")
    me = row * col_count + col
    core = lax.rem(col, 2)
    chip = row * half_cols + col // 2
    partner = (col + 1 - 2 * core, row)

    def device(index):
        return (lax.rem(index, col_count), index // col_count)

    def remote(src, dst, kind, target):
        return pltpu.make_async_remote_copy(
            src_ref=src, dst_ref=dst, send_sem=send_sem.at[kind], recv_sem=recv_sem.at[kind],
            device_id=target, device_id_type=MESH,
        )

    def to_all(make):
        def step(distance, carry):
            make(lax.rem(me + distance, count)).start()
            return carry
        lax.fori_loop(1, count, step, 0)

    def to_rows(make):
        def step(distance, carry):
            make(lax.rem(row + distance, row_count)).start()
            return carry
        lax.fori_loop(1, row_count, step, 0)

    def wait_for(ref, sem, kind):
        pltpu.make_async_copy(ref, ref, sem.at[kind]).wait()

    barrier = pltpu.get_barrier_semaphore()

    def greet(distance, carry):
        pl.semaphore_signal(
            barrier, inc=1, device_id=device(lax.rem(me + distance, count)), device_id_type=MESH
        )
        return carry

    lax.fori_loop(1, count, greet, 0)

    for load in loads[:4]:
        load.wait()
    for slot in range(cols):
        cell_send[slot, :rows, :] = pair_ref[:, slot, :]
        cell_send[slot, rows:, :] = cot_ref[:, slot, :]
    gain = gain_ref[...]
    block_scaled, block_inverse = layer_norm_parts(pair_ref[...].reshape(rows * cols, width))
    spread_bias = jnp.broadcast_to(wb_ref[...][:, None, :], (heads, tokens, width)).reshape(
        heads * tokens, width
    )
    products = dot(block_scaled * gain, spread_bias, 1, 1).reshape(rows, cols, heads * tokens)
    lane_token = lax.broadcasted_iota(jnp.int32, (1, cols, heads * tokens), 2) & (tokens - 1)
    block_col = lax.broadcasted_iota(jnp.int32, (1, cols, heads * tokens), 1) + col * cols
    own_lane = lane_token == block_col
    bias_send[...] = jnp.sum(jnp.where(own_lane, products, 0.0), axis=1)
    pl.semaphore_wait(barrier, count - 1)

    to_rows(lambda r: remote(cell_send.at[r], cell_recv.at[row], CELLS, (col, r)))
    to_all(lambda d: remote(bias_send, bias_recv.at[me], BIAS, device(d)))
    cell_recv[row] = cell_send[row]
    bias_recv[me] = bias_send[...]

    for load in loads[4:]:
        load.wait()
    own = col * cols + row
    token_shift = (tokens // blocks).bit_length() - 1
    chain_row = chain_ref[...].astype(jnp.float32)
    square_row = lax.broadcasted_iota(jnp.int32, (tokens, tokens), 0)
    square_col = lax.broadcasted_iota(jnp.int32, (tokens, tokens), 1)
    chain_all = jnp.broadcast_to(chain_row, (tokens, tokens))
    chain_col = jnp.sum(jnp.where(square_row == square_col, chain_all, 0.0), axis=1, keepdims=True)
    own_chain = jnp.sum(jnp.where(square_col == own, chain_all, 0.0), axis=1, keepdims=True)
    spread_row = (
        lax.broadcasted_iota(jnp.int32, (tokens, blocks), 0) >> token_shift
        == lax.broadcasted_iota(jnp.int32, (tokens, blocks), 1)
    ).astype(jnp.float32)
    spread_template = dot(spread_row, template_ref[...].astype(jnp.float32))
    block_lane = lax.broadcasted_iota(jnp.int32, (tokens, blocks), 1)
    template_col = jnp.sum(
        jnp.where(block_lane == own >> token_shift, spread_template, 0.0), axis=1, keepdims=True
    )
    keep = (chain_col == own_chain) | (template_col > 0.5)
    depth_shift = depth.bit_length() - 1
    head_mask = (
        lax.broadcasted_iota(jnp.int32, (heads, 1, width), 2) >> depth_shift
        == lax.broadcasted_iota(jnp.int32, (heads, 1, width), 0)
    ).astype(jnp.float32)

    def by_head(array):
        return (array[None] * head_mask).reshape(heads * tokens, width)

    def own_head(array):
        return jnp.sum(array.reshape(heads, tokens, width) * head_mask, axis=0)

    wait_for(cell_recv.at[pl.ds(0, row_count - 1)], recv_sem, CELLS)
    cells = jnp.concatenate([cell_recv[r, :rows, :] for r in range(row_count)], axis=0)
    upstream = jnp.concatenate([cell_recv[r, rows:, :] for r in range(row_count)], axis=0)
    scaled, inverse = layer_norm_parts(cells)
    normed = scaled * gain
    queries = dot(normed, wq_ref[...])
    keys = dot(normed, wk_ref[...])
    values = dot(normed, wv_ref[...])
    gate = jax.nn.sigmoid(dot(normed, wg_ref[...]) + gate_bias_ref[...])
    d_gated = dot(upstream, wo_ref[...], 1, 1)
    d_attended_heads = by_head(d_gated * gate)
    query_heads = by_head(queries)
    scores = dot(keys, query_heads, 1, 1) * factor
    d_weights = dot(values, d_attended_heads, 1, 1)

    wait_for(bias_recv.at[pl.ds(0, count - 1)], recv_sem, BIAS)
    bias_rows = jnp.sum(bias_recv[...].reshape(row_count, col_count, rows, heads * tokens), axis=1)
    for r in range(row_count):
        bias_full[r * rows : (r + 1) * rows, :] = bias_rows[r]
    scores = jnp.where(keep, scores + bias_full[...], NEG_FILL)
    weights = jnp.exp(scores - jnp.max(scores, axis=0, keepdims=True))
    weights = weights / jnp.sum(weights, axis=0, keepdims=True)
    d_scores = weights * (d_weights - jnp.sum(weights * d_weights, axis=0, keepdims=True))
    for r in range(row_count):
        score_send[r] = d_scores[r * rows : (r + 1) * rows, :]
    to_all(lambda d: remote(score_send.at[d // col_count], score_recv.at[me], SCORE_GRAD, device(d)))
    score_recv[me] = score_send[row]

    def share(index, grad):
        parts[index] = grad
        owner = 0 if index < CORE_SETS[0][1] else 1

        @pl.when(core != owner)
        def _():
            remote(parts.at[index], pair_recv.at[index], PAIR + index, partner).start()

    attended = own_head(dot(weights, values, 0, 0))
    gated = gate * attended
    d_gate = d_gated * attended * gate * (1.0 - gate)
    d_query = own_head(dot(d_scores, keys, 0, 0)) * factor
    d_key = dot(d_scores, query_heads) * factor
    d_value = dot(weights, d_attended_heads)
    share(3, dot(normed, d_query, 0, 0))
    share(4, dot(normed, d_key, 0, 0))
    share(0, dot(gated, upstream, 0, 0))
    share(1, dot(normed, d_gate, 0, 0))
    share(2, dot(normed, d_value, 0, 0))

    for which in range(2):
        first, number = CORE_SETS[which]

        @pl.when(core == which)
        def _(first=first, number=number):
            for index in range(first, first + number):
                wait_for(pair_recv.at[index], recv_sem, PAIR + index)
                parts[index] = parts[index] + pair_recv[index]

            def step(distance, carry):
                target = lax.rem(chip + distance, chips)
                remote(
                    parts.at[pl.ds(first, number), pl.ds(pl.multiple_of(target * tile, tile), tile), :],
                    scatter_recv.at[chip, pl.ds(0, number)],
                    SCATTER,
                    (lax.rem(target, half_cols) * 2 + core, target // half_cols),
                ).start()
                return carry

            lax.fori_loop(1, chips, step, 0)

    d_normed = (
        dot(d_query, wq_ref[...], 1, 1)
        + dot(d_key, wk_ref[...], 1, 1)
        + dot(d_value, wv_ref[...], 1, 1)
        + dot(d_gate, wg_ref[...], 1, 1)
    )
    d_cells = layer_norm_back(d_normed * gain, scaled, inverse)
    for r in range(row_count):
        grad_send[r] = d_cells[r * rows : (r + 1) * rows, :]
    to_rows(lambda r: remote(grad_send.at[r], grad_recv.at[row], CELL_GRAD, (col, r)))
    grad_recv[row] = grad_send[row]
    update = dot(gated, wo_ref[...])
    for r in range(row_count):
        update_send[r] = update[r * rows : (r + 1) * rows, :]
    to_rows(lambda r: remote(update_send.at[r], update_recv.at[row], UPDATE, (col, r)))
    update_recv[row] = update_send[row]

    wait_for(score_recv.at[pl.ds(0, count - 1)], recv_sem, SCORE_GRAD)
    bias_grad = jnp.sum(score_recv[...], axis=0)
    picked = jnp.where(own_lane, bias_grad[:, None, :], 0.0).reshape(rows * cols, heads * tokens)
    bias_sums = dot(picked, block_scaled, 0, 0).reshape(heads, tokens, width)
    small_send[0:heads, :] = jnp.sum(bias_sums, axis=1)
    small_send[heads : heads + 1, :] = jnp.sum(d_gate, axis=0, keepdims=True)
    small_send[heads + 1 : heads + 2, :] = jnp.sum(d_normed * scaled, axis=0, keepdims=True)
    to_all(lambda d: remote(small_send, small_recv.at[me], SMALL, device(d)))
    small_recv[me] = small_send[...]
    bias_part = layer_norm_back(dot(picked, spread_bias) * gain, block_scaled, block_inverse).reshape(
        rows, cols, width
    )

    share_scale = 1.0 / tokens
    for which in range(2):
        first, number = CORE_SETS[which]

        @pl.when(core == which)
        def _(first=first, number=number):
            mine = pl.ds(pl.multiple_of(chip * tile, tile), tile)
            wait_for(scatter_recv.at[pl.ds(0, chips - 1), pl.ds(0, number)], recv_sem, SCATTER)
            scatter_recv[chip, pl.ds(0, number)] = parts[pl.ds(first, number), mine, :]
            total = jnp.sum(scatter_recv[:, pl.ds(0, number)], axis=0) * share_scale
            gather_send[pl.ds(0, number)] = total
            final[pl.ds(first, number), mine, :] = total

            def step(distance, carry):
                target = lax.rem(chip + distance, chips)
                remote(
                    gather_send.at[pl.ds(0, number)],
                    final.at[pl.ds(first, number), mine, :],
                    GATHER,
                    (lax.rem(target, half_cols) * 2 + core, target // half_cols),
                ).start()
                return carry

            lax.fori_loop(1, chips, step, 0)

    wait_for(grad_recv.at[pl.ds(0, row_count - 1)], recv_sem, CELL_GRAD)
    wait_for(update_recv.at[pl.ds(0, row_count - 1)], recv_sem, UPDATE)
    for slot in range(cols):
        pair_out[:, slot, :] = grad_recv[slot] + bias_part[:, slot, :]
        update_out[:, slot, :] = update_recv[slot]
    store(pair_out, pair_hbm)
    store(update_out, update_hbm)
    wait_for(small_recv.at[pl.ds(0, count - 1)], recv_sem, SMALL)
    small = jnp.sum(small_recv[...], axis=0) * share_scale
    bias_out[...] = small[:heads] * gain
    gate_bias_out[...] = small[heads : heads + 1]
    gain_out[...] = small[heads + 1 : heads + 2] + jnp.sum(
        small[:heads] * wb_ref[...], axis=0, keepdims=True
    )
    store(bias_out, bias_hbm)
    store(gate_bias_out, gate_bias_hbm)
    store(gain_out, gain_hbm)

    for which in range(2):
        first, number = CORE_SETS[which]
        other_first, other_number = CORE_SETS[1 - which]

        @pl.when(core == which)
        def _(first=first, number=number, other_first=other_first, other_number=other_number):
            some = scatter_recv.at[pl.ds(0, chips - 1), pl.ds(0, number)]
            wait_for(some, recv_sem, GATHER)
            forward = final.at[pl.ds(first, number)]
            remote(forward, forward, FORWARD, partner).start()
            wait_for(final.at[pl.ds(other_first, other_number)], recv_sem, FORWARD)
            wait_for(some, send_sem, SCATTER)
            wait_for(some, send_sem, GATHER)
            wait_for(forward, send_sem, FORWARD)
            for index in range(other_first, other_first + other_number):
                wait_for(parts.at[index], send_sem, PAIR + index)

    for index, target in enumerate((wo_hbm, gate_hbm, value_hbm, query_hbm, key_hbm)):
        store(final.at[index], target)
    wait_for(cell_recv.at[pl.ds(0, row_count - 1)], send_sem, CELLS)
    wait_for(bias_recv.at[pl.ds(0, count - 1)], send_sem, BIAS)
    wait_for(update_recv.at[pl.ds(0, row_count - 1)], send_sem, UPDATE)
    wait_for(grad_recv.at[pl.ds(0, row_count - 1)], send_sem, CELL_GRAD)
    wait_for(score_recv.at[pl.ds(0, count - 1)], send_sem, SCORE_GRAD)
    wait_for(small_recv.at[pl.ds(0, count - 1)], send_sem, SMALL)
    for copy in stores:
        copy.wait()


def store_kernel(*refs):
    copies = [
        pltpu.make_async_copy(refs[index], refs[10 + index], refs[20].at[index]) for index in range(10)
    ]
    for copy in copies:
        copy.start()
    for copy in copies:
        copy.wait()


def body_fused(
    row_count, col_count, tokens,
    pair_rep, cotangent, chain_ids, template, norm_gain,
    w_query, w_key, w_value, w_gate, gate_bias, w_out, w_bias,
):
    rows, cols, width = pair_rep.shape
    heads = w_bias.shape[0]
    count = row_count * col_count
    chips = count // 2
    tile = width // chips
    number = CORE_SETS[0][1]
    f32 = jnp.float32
    arrays = (
        pair_rep, cotangent, chain_ids.reshape(1, -1), template, norm_gain.reshape(1, -1),
        w_query, w_key, w_value, w_gate, gate_bias.reshape(1, -1), w_out, w_bias,
    )

    def shape(*dims):
        return jax.ShapeDtypeStruct(dims, f32)

    def vmem(*dims):
        return pltpu.VMEM(dims, f32)

    square = shape(width, width)
    out = pl.pallas_call(
        functools.partial(fused_kernel, row_count, col_count, tokens, heads, template.shape[0]),
        out_shape=(
            shape(rows, cols, width), shape(rows, cols, width), square, square, square, square,
            shape(1, width), square, shape(heads, width), shape(1, width),
        ),
        in_specs=[pl.BlockSpec(memory_space=pltpu.HBM)] * 12,
        out_specs=[pl.BlockSpec(memory_space=pltpu.HBM)] * 10,
        scratch_shapes=[
            vmem(cols, 2 * rows, width), vmem(row_count, 2 * rows, width),
            vmem(rows, width), vmem(count, rows, width), vmem(tokens, width),
            vmem(row_count, rows, width), vmem(row_count, rows, width),
            vmem(row_count, rows, width), vmem(row_count, rows, width),
            vmem(row_count, rows, width), vmem(count, rows, width),
            vmem(heads + 2, width), vmem(count, heads + 2, width),
            vmem(MATRICES, width, width), vmem(MATRICES, width, width),
            vmem(chips, number, tile, width), vmem(number, tile, width), vmem(MATRICES, width, width),
            *[pltpu.VMEM(array.shape, array.dtype) for array in arrays],
            vmem(rows, cols, width), vmem(rows, cols, width),
            vmem(heads, width), vmem(1, width), vmem(1, width),
            pltpu.SemaphoreType.DMA((PAIR + MATRICES,)),
            pltpu.SemaphoreType.DMA((PAIR + MATRICES,)),
            pltpu.SemaphoreType.DMA((len(arrays),)),
            pltpu.SemaphoreType.DMA((10,)),
        ],
        compiler_params=pltpu.CompilerParams(
            collective_id=0, has_side_effects=True, vmem_limit_bytes=63 * 1024 * 1024
        ),
        name="triangle",
    )(*arrays)
    out = pl.pallas_call(
        store_kernel,
        out_shape=[jax.ShapeDtypeStruct(array.shape, array.dtype) for array in out],
        in_specs=[pl.BlockSpec(memory_space=pltpu.HBM)] * 10,
        out_specs=[pl.BlockSpec(memory_space=pltpu.HBM)] * 10,
        scratch_shapes=[pltpu.SemaphoreType.DMA((10,))],
        compiler_params=pltpu.CompilerParams(vmem_limit_bytes=63 * 1024 * 1024),
        name="store",
    )(*out)
    return tuple(out[:6]) + (out[6].reshape(width),) + tuple(out[7:9]) + (out[9].reshape(width),)


def body(*arrays):
    row_count, col_count = lax.axis_size("row"), lax.axis_size("col")
    rows, cols, width = arrays[0].shape
    tokens = rows * row_count
    heads = arrays[11].shape[0]
    chips = row_count * col_count // 2
    fits = heads * tokens == LANES and width == LANES and width % (chips * SUBLANES) == 0
    if fits and cols == row_count and col_count % 2 == 0:
        return body_fused(row_count, col_count, tokens, *arrays)
    return body_collective(*arrays)


def solution(mesh):
    in_specs = (
        P("row", "col", None),
        P("row", "col", None),
        P(),
        P(),
        P(),
        P(),
        P(),
        P(),
        P(),
        P(),
        P(),
        P(),
    )
    out_specs = (
        P("row", "col", None),
        P("row", "col", None),
        P(),
        P(),
        P(),
        P(),
        P(),
        P(),
        P(),
        P(),
    )
    return jax.shard_map(body, mesh=mesh, in_specs=in_specs, out_specs=out_specs, check_vma=False)
```
